32 devices in a mesh: lev: 4 (over x, core), hor: 8 (over z, y).
Axes of the slice: x: 2, y: 2, z: 4, core: 2. Of those that a mesh axis runs over, the one named last changes fastest.
Arguments:
- state: float32 [2, 128, 128, 1024], P(None, 'lev', 'hor'), may hold values from -6 to 6
- cotangent: bfloat16 [2, 128, 128, 1024], P(None, 'lev', 'hor'), may hold values from -6 to 6
- diffusion: float32 [128, 128, 1024], P('lev', 'hor'), may hold values from 0.02 to 0.2
- vertical_inverse: float32 [2, 128, 128], replicated, may hold values from -0.2 to 2
- w_in: bfloat16 [1024, 256], replicated, may hold values from -0.375 to 0.375
- w_out: bfloat16 [256, 1024], replicated, may hold values from -0.1875 to 0.1875
Outputs:
- state_adjoint: float32 [2, 128, 128, 1024], P(None, 'lev', 'hor')
The draws below stay inside these ranges and needn't reach their ends.
All inputs are finite; a program needn't handle non-finite values.
Results may differ from the reference program's by a relative error of at most 0.002.
Values may be sent and summed in bfloat16 or wider, within the bound.
No kernel may reach another device: no remote copies, remote signals or barrier semaphores. Data moves between devices by JAX's collectives and lax.ppermute only.
A program may use at most 64 MiB of HBM per device.

```python
import math
import jax
import jax.numpy as jnp
from jax import lax

FIELDS = 2
LEV = 128
HID = 1024
NY = 1024
NX = 128
FEAT = 256


def draw_vertical_inverse(key, part):
    key_off = jax.random.fold_in(key, 11)
    key_diag = jax.random.fold_in(key, 23)
    offdiag = jnp.clip(0.05 * jax.random.normal(key_off, (FIELDS, LEV, LEV), jnp.float32), -0.2, 0.2)
    diag_values = jax.random.uniform(key_diag, (FIELDS, LEV), jnp.float32, 1.0, 2.0)
    identity = jnp.eye(LEV, dtype=jnp.float32)
    return offdiag * (1.0 - identity) + identity * diag_values[:, :, None]


def steps_of(key, extent, cuts, low, top_value):
    def one(axis_at, parts):
        draws = jax.random.uniform(jax.random.fold_in(jax.random.fold_in(key, 6), axis_at), (parts,), jnp.float32, low / len(cuts), top_value / len(cuts))
        return jnp.repeat(jnp.exp(draws), extent[axis_at] // parts).reshape((-1,) + (1,) * (len(extent) - axis_at - 1))

    factor_of = one(*cuts[0])
    for cut in cuts[1:]:
        factor_of = factor_of * one(*cut)
    return factor_of


def gaussian(key, extent, deviation, bound, cuts=(), held_as=jnp.bfloat16):
    drawn = jax.random.normal(key, extent, jnp.float32) * deviation
    if len(cuts) > 0:
        drawn = steps_of(key, extent, cuts, -0.22, 0.18) * drawn
    return jnp.clip(drawn, min=-bound, max=bound).astype(held_as)


def setup_inputs(seed: int = 0) -> dict:
    streams_of = jax.random.split(jax.random.key(seed), 7)
    state = gaussian(streams_of[0], (FIELDS, LEV, NX, NY), 1.0, 6.0, ((1, 4), (2, 8)), jnp.float32)
    cotangent = gaussian(streams_of[1], (FIELDS, LEV, NX, NY), 1.0, 6.0, ((1, 4), (2, 8)))
    diffusion = jnp.clip(jnp.exp(math.log(0.2) - 2.3025851 * jax.random.uniform(streams_of[2], (LEV, NX, NY), jnp.float32) ** steps_of(streams_of[2], (LEV, NX, NY), ((0, 4), (1, 8)), -0.2, 0.2)), 0.02, 0.2)
    vertical_inverse = draw_vertical_inverse(jax.random.fold_in(streams_of[6], 71), 0)
    w_in = gaussian(streams_of[4], (HID, FEAT), FEAT ** -0.5, 0.375)
    w_out = gaussian(streams_of[5], (FEAT, HID), HID ** -0.5, 0.1875)
    return {"state": state, "cotangent": cotangent, "diffusion": diffusion, "vertical_inverse": vertical_inverse, "w_in": w_in, "w_out": w_out}


def laplace(field):
    padded = jnp.pad(field, ((0, 0), (0, 0), (1, 1), (1, 1)))
    return (padded[:, :, 2:, 1:-1] + padded[:, :, :-2, 1:-1] + padded[:, :, 1:-1, 2:]
            + padded[:, :, 1:-1, :-2] - 4.0 * padded[:, :, 1:-1, 1:-1])


def column_adjoint(diffused, cot_block, vertical_inverse, w_in, w_out):
    highest = lax.Precision.HIGHEST
    solved = jnp.einsum("fkl,flc->fkc", vertical_inverse, diffused, precision=highest)
    fields, levels, count = solved.shape
    inputs = solved.reshape(fields * levels, count).astype(jnp.bfloat16)
    preact = jnp.dot(w_in, inputs, preferred_element_type=jnp.float32)
    cot_cols = cot_block.reshape(fields * levels, count)
    hidden_grad = lax.dot_general(w_out, cot_cols, (((0,), (0,)), ((), ())), preferred_element_type=jnp.float32)
    squashed = jax.nn.sigmoid(preact)
    pre_grad = (hidden_grad * squashed * (1.0 + preact * (1.0 - squashed))).astype(jnp.bfloat16)
    level_grad = cot_cols.astype(jnp.float32) + lax.dot_general(w_in, pre_grad, (((0,), (0,)), ((), ())), preferred_element_type=jnp.float32)
    level_grad = level_grad.reshape(fields, levels, count)
    return jnp.einsum("fkl,fkc->flc", vertical_inverse, level_grad, precision=highest)


def reference(state, cotangent, diffusion, vertical_inverse, w_in, w_out):
    diffused = state + diffusion[None] * laplace(state)
    rows_first = jnp.moveaxis(diffused, 2, 0)
    cot_first = jnp.moveaxis(cotangent, 2, 0)

    def one_row(pair):
        return column_adjoint(pair[0], pair[1], vertical_inverse, w_in, w_out)

    adjoint_rows = lax.map(one_row, (rows_first, cot_first))
    adjoint_diffused = jnp.moveaxis(adjoint_rows, 0, 2)
    return adjoint_diffused + laplace(diffusion[None] * adjoint_diffused)
```

```python
import functools

import jax
import jax.numpy as jnp
from jax import lax
from jax.experimental import pallas as pl
from jax.experimental.pallas import tpu as pltpu
from jax.sharding import PartitionSpec as P

F32, BF16 = jnp.float32, jnp.bfloat16
PARAMS = pltpu.CompilerParams(vmem_limit_bytes=48 * 1024 * 1024)
SMEM = pl.BlockSpec(memory_space=pltpu.SMEM)


def row_table(rows, count):
    half = rows // 2
    order = []
    for row in [0, rows - 1, half - 1, half] + list(range(rows)):
        if row not in order:
            order.append(row)
    return [order[c * count : (c + 1) * count] for c in range(rows // count)]


def pick(values, at):
    out = jnp.int32(values[0])
    for i, value in enumerate(values[1:], 1):
        out = jnp.where(at == i, jnp.int32(value), out)
    return out


def link_type(distance):
    return F32 if distance < 2 else BF16


def lateral(row):
    width = row.shape[1]
    lane = lax.broadcasted_iota(jnp.int32, row.shape, 1)
    left = jnp.where(lane == 0, 0.0, pltpu.roll(row, 1, 1))
    right = jnp.where(lane == width - 1, 0.0, pltpu.roll(row, width - 1, 1))
    return left + right


LANES = 128


def spread(held, x):
    for t in range(held.shape[0]):
        held[t] = x[:, t * LANES : (t + 1) * LANES]


def gather_rows(held, row, count, stride):
    return jnp.concatenate(
        [held[t, pl.ds(row, count, stride=stride), :] for t in range(held.shape[0])], axis=1
    )


def cot_kernel(table, count, rows, me_ref, cot_ref, *refs):
    outs, held = refs[:count], refs[count]
    me = me_ref[0]
    levels = cot_ref.shape[1]
    for f in range(cot_ref.shape[0]):
        spread(held, cot_ref[f].astype(F32).reshape(levels * rows, cot_ref.shape[3]))
        for k in range(count):
            for c, order in enumerate(table):
                row = pick(order, me ^ k)
                outs[k][c, f] = gather_rows(held, row, levels, rows).astype(BF16)


def split_cot(me, cot, table, count):
    fields, levels, rows, width = cot.shape
    step = min(levels, 16)
    chunks = len(table)
    out = jax.ShapeDtypeStruct((chunks, fields, levels, width), BF16)
    return pl.pallas_call(
        functools.partial(cot_kernel, table, count, rows),
        out_shape=[out] * count,
        grid=(levels // step,),
        in_specs=[SMEM, pl.BlockSpec((fields, step, rows, width), lambda i: (0, i, 0, 0))],
        out_specs=[pl.BlockSpec((chunks, fields, step, width), lambda i: (0, 0, i, 0))] * count,
        scratch_shapes=[pltpu.VMEM((width // LANES, step * rows, LANES), F32)],
        compiler_params=PARAMS,
        cost_estimate=pl.CostEstimate(flops=0, bytes_accessed=4 * cot.size, transcendentals=0),
        name="split_cot",
    )(me, cot)


def diffuse_kernel(table, count, rows, me_ref, state_ref, diff_ref, low_ref, high_ref, *refs):
    chunks = len(table)
    outs, (held, state_held, diff_held) = refs[: chunks * count], refs[chunks * count :]
    me = me_ref[0]
    levels = low_ref.shape[1]
    spread(diff_held, diff_ref[...])
    for f in range(low_ref.shape[0]):
        spread(state_held, state_ref[f])

        def line(r):
            if r < 0:
                return low_ref[f]
            if r == rows:
                return high_ref[f]
            return gather_rows(state_held, r, levels, rows)

        before, here = line(-1), line(0)
        for r in range(rows):
            after = line(r + 1)
            total = before + after + lateral(here) - 4.0 * here
            held[r] = here + gather_rows(diff_held, r, levels, rows) * total
            before, here = here, after
        for c, order in enumerate(table):
            for k in range(count):
                out = outs[c * count + k]
                out[f] = held[pick(order, me ^ k)].astype(out.dtype)


def diffuse(me, state, diffusion, low, high, table, count):
    fields, levels, rows, width = state.shape
    step = min(levels, 16)
    slab = pl.BlockSpec((fields, step, width), lambda i: (0, i, 0))
    shapes = [
        jax.ShapeDtypeStruct((fields, levels, width), link_type(k)) for _ in table for k in range(count)
    ]
    outs = pl.pallas_call(
        functools.partial(diffuse_kernel, table, count, rows),
        out_shape=shapes,
        grid=(levels // step,),
        in_specs=[
            SMEM,
            pl.BlockSpec((fields, step * rows, width), lambda i: (0, i, 0)),
            pl.BlockSpec((step * rows, width), lambda i: (i, 0)),
            slab,
            slab,
        ],
        out_specs=[slab] * len(shapes),
        scratch_shapes=[pltpu.VMEM((rows, step, width), F32)]
        + [pltpu.VMEM((width // LANES, step * rows, LANES), F32)] * 2,
        compiler_params=PARAMS,
        cost_estimate=pl.CostEstimate(flops=10 * state.size, bytes_accessed=9 * state.size, transcendentals=0),
        name="diffuse",
    )(me, state.reshape(fields, levels * rows, width), diffusion.reshape(levels * rows, width), low, high)
    return [outs[c * count : (c + 1) * count] for c in range(len(table))]


def dot(a, b):
    return jnp.dot(a, b, preferred_element_type=F32)


def halves(x):
    top = x.astype(BF16)
    return top, (x - top.astype(F32)).astype(BF16)


def vertical(matrix, x):
    m_top, m_rest = halves(matrix)
    x_top, x_rest = halves(x)
    return dot(m_top, x_top) + (dot(m_rest, x_top) + dot(m_top, x_rest))


def column_kernel(count, me_ref, *refs):
    fields, lev, _ = refs[2 * count].shape
    states, cots = refs[:count], refs[count : 2 * count]
    v_ref, vt_ref, win_ref, wint_ref, woutt_ref = refs[2 * count : 2 * count + 5]
    outs = refs[2 * count + 5 : 3 * count + 5]
    cols, cot_cols, back = refs[3 * count + 5 :]
    me = me_ref[0]
    levels = lev // count
    for k in range(count):
        at = pl.ds(pl.multiple_of((me ^ k) * levels, levels), levels)
        for f in range(fields):
            cols[f, at, :] = states[k][f].astype(F32)
            cot_cols[f, at, :] = cots[k][f].astype(F32)
    inputs = jnp.concatenate(
        [vertical(v_ref[f], cols[f]).astype(BF16) for f in range(fields)], axis=0
    )
    cot = jnp.concatenate([cot_cols[f] for f in range(fields)], axis=0)
    cot_half = cot.astype(BF16)
    hidden, block = win_ref.shape[0], 256
    grad = cot
    for h in range(0, hidden, block):
        preact = dot(win_ref[h : h + block, :], inputs)
        hidden_grad = dot(woutt_ref[h : h + block, :], cot_half)
        s = 0.5 + 0.5 * jnp.tanh(0.5 * preact)
        pre_grad = (hidden_grad * s * (1.0 + preact * (1.0 - s))).astype(BF16)
        grad = grad + dot(wint_ref[:, h : h + block], pre_grad)
    for f in range(fields):
        back[f] = vertical(vt_ref[f], grad[f * lev : (f + 1) * lev])
    for k in range(count):
        at = pl.ds(pl.multiple_of((me ^ k) * levels, levels), levels)
        for f in range(fields):
            outs[k][f] = back[f, at, :].astype(outs[k].dtype)


def columns(me, states, cots, chunk, v, vt, w_in, w_in_t, w_out_t):
    count = len(states)
    fields, levels, width = states[0].shape
    lev = v.shape[1]
    tile = min(width, 512)
    slab = pl.BlockSpec((fields, levels, tile), lambda i: (0, 0, i))
    cot_slab = pl.BlockSpec((None, fields, levels, tile), lambda i: (chunk, 0, 0, i))

    def whole(x):
        return pl.BlockSpec(x.shape, lambda i: (0,) * x.ndim)

    feat, hidden = w_in_t.shape
    return pl.pallas_call(
        functools.partial(column_kernel, count),
        out_shape=[jax.ShapeDtypeStruct((fields, levels, width), link_type(k)) for k in range(count)],
        grid=(width // tile,),
        in_specs=[SMEM] + [slab] * count + [cot_slab] * count + [whole(x) for x in (v, vt, w_in, w_in_t, w_out_t)],
        out_specs=[slab] * count,
        scratch_shapes=[pltpu.VMEM((fields, lev, tile), F32)] * 3,
        compiler_params=PARAMS,
        cost_estimate=pl.CostEstimate(
            flops=6 * feat * hidden * width * 2,
            bytes_accessed=10 * feat * width,
            transcendentals=hidden * width,
        ),
        name=f"columns_{chunk}",
    )(me, *states, *cots, v, vt, w_in, w_in_t, w_out_t)


def edge_kernel(table, count, rows, me_ref, first_ref, last_ref, *refs):
    pieces, low, high = refs[:count], refs[count], refs[count + 1]
    me = me_ref[0]
    for k in range(count):
        row = pick(table[0], me ^ k)

        @pl.when(row == 0)
        def _():
            for f in range(low.shape[0]):
                low[f] = first_ref[...] * pieces[k][f].astype(F32)

        @pl.when(row == rows - 1)
        def _():
            for f in range(low.shape[0]):
                high[f] = last_ref[...] * pieces[k][f].astype(F32)


def edges(me, first, last, pieces, table, rows):
    shape = jax.ShapeDtypeStruct(pieces[0].shape, F32)
    return pl.pallas_call(
        functools.partial(edge_kernel, table, len(pieces), rows),
        out_shape=[shape] * 2,
        in_specs=[SMEM] + [pl.BlockSpec(memory_space=pltpu.VMEM)] * (2 + len(pieces)),
        out_specs=[pl.BlockSpec(memory_space=pltpu.VMEM)] * 2,
        compiler_params=PARAMS,
        cost_estimate=pl.CostEstimate(flops=0, bytes_accessed=4 * 4 * shape.size, transcendentals=0),
        name="edges",
    )(me, first, last, *pieces)


def final_kernel(table, count, rows, top, aliased, me_ref, diff_ref, low_ref, high_ref, *refs):
    chunks = len(table)
    pieces = refs[: chunks * count]
    out, held, diff_held, out_held = refs[chunks * count + aliased :]
    me = me_ref[0]
    levels = low_ref.shape[1]
    spread(diff_held, diff_ref[...])
    span = out.shape[1] // levels
    start = top * span
    for f in range(low_ref.shape[0]):
        for c, order in enumerate(table):
            for k in range(count):
                held[pick(order, me ^ k)] = pieces[c * count + k][f].astype(F32)

        def weighted(r):
            if r < 0:
                return low_ref[f]
            if r == rows:
                return high_ref[f]
            return held[r] * gather_rows(diff_held, r, levels, rows)

        before, here = weighted(start - 1), weighted(start)
        for r in range(start, start + span):
            after = weighted(r + 1)
            total = before + after + lateral(here) - 4.0 * here
            value = held[r] + total
            for t in range(out_held.shape[0]):
                at = pl.ds(r - start, levels, stride=span)
                out_held[t, at, :] = value[:, t * LANES : (t + 1) * LANES]
            before, here = here, after
        for t in range(out_held.shape[0]):
            out[f, :, t * LANES : (t + 1) * LANES] = out_held[t]


def final(me, diffusion, low, high, pieces, table, top, base):
    count = len(pieces[0])
    fields, levels, width = low.shape
    rows = diffusion.shape[1]
    span = rows // 2
    step = min(levels, 16)
    slab = pl.BlockSpec((fields, step, width), lambda i: (0, i, 0))
    needed = [piece for chunk in pieces for piece in chunk]
    out = jax.ShapeDtypeStruct((fields, levels, rows, width), F32)
    block = pl.BlockSpec((fields, step, span, width), lambda i: (0, i, top, 0))
    aliased = base is not None

    def kernel(*refs):
        refs = list(refs)
        at = 4 + len(needed) + aliased
        refs[at] = refs[at].reshape(fields, step * span, width)
        final_kernel(table[: len(pieces)], count, rows, top, aliased, *refs)

    return pl.pallas_call(
        kernel,
        out_shape=out,
        grid=(levels // step,),
        in_specs=[SMEM, pl.BlockSpec((step * rows, width), lambda i: (i, 0)), slab, slab]
        + [slab] * len(needed)
        + ([pl.BlockSpec(memory_space=pl.ANY)] if aliased else []),
        out_specs=block,
        scratch_shapes=[
            pltpu.VMEM((rows, step, width), F32),
            pltpu.VMEM((width // LANES, step * rows, LANES), F32),
            pltpu.VMEM((width // LANES, step * span, LANES), F32),
        ],
        input_output_aliases={4 + len(needed): 0} if aliased else {},
        compiler_params=PARAMS,
        cost_estimate=pl.CostEstimate(flops=0, bytes_accessed=6 * out.size, transcendentals=0),
        name=f"final_{top}",
    )(me, diffusion.reshape(levels * rows, width), low, high, *needed, *([base] if aliased else []))


def swap(x, distance, count):
    if distance == 0:
        return x
    return lax.ppermute(x, "lev", [(i, i ^ distance) for i in range(count)])


def halo(first, last):
    count = lax.axis_size("hor")
    forward = [(i, i + 1) for i in range(count - 1)]
    backward = [(target, source) for source, target in forward]
    return lax.ppermute(last, "hor", forward), lax.ppermute(first, "hor", backward)


def body(state, cotangent, diffusion, vertical_inverse, w_in, w_out):
    count = lax.axis_size("lev")
    rows = state.shape[2]
    table = row_table(rows, count)
    chunks = len(table)
    me = lax.axis_index("lev").astype(jnp.int32).reshape(1)

    cots = [swap(x, k, count) for k, x in enumerate(split_cot(me, cotangent, table, count))]
    low, high = halo(state[:, :, 0], state[:, :, rows - 1])
    sent = diffuse(me, state, diffusion, low, high, table, count)
    v_t = vertical_inverse.transpose(0, 2, 1)
    first, last = diffusion[:, 0], diffusion[:, rows - 1]
    returned = []
    for c in range(chunks):
        states = [swap(x, k, count) for k, x in enumerate(sent[c])]
        out = columns(me, states, cots, c, vertical_inverse, v_t, w_in, w_in.T, w_out.T)
        returned.append([swap(x, k, count) for k, x in enumerate(out)])
    low, high = halo(*edges(me, first, last, returned[0], table, rows))
    span = rows // 2
    chunk_of = {row: c for c, order in enumerate(table) for row in order}
    needed = 1 + max(chunk_of[row] for row in range(span + 1))
    result = final(me, diffusion, low, high, returned[:needed], table, 0, None)
    return final(me, diffusion, low, high, returned, table, 1, result)


def solution(mesh):
    placed = (
        P(None, "lev", "hor", None),
        P(None, "lev", "hor", None),
        P("lev", "hor", None),
        P(),
        P(),
        P(),
    )
    return jax.shard_map(
        body, mesh=mesh, in_specs=placed, out_specs=P(None, "lev", "hor", None), check_vma=False
    )
```

```python
import functools

import jax
import jax.numpy as jnp
from jax import lax
from jax.experimental import pallas as pl
from jax.experimental.pallas import tpu as pltpu
from jax.sharding import PartitionSpec as P

F32, BF16 = jnp.float32, jnp.bfloat16
VMEM_MIB = 20
PARAMS = pltpu.CompilerParams(vmem_limit_bytes=VMEM_MIB * 1024 * 1024)
COST = pl.CostEstimate(flops=1, bytes_accessed=1, transcendentals=0)
COLUMN_COST = pl.CostEstimate(flops=1, bytes_accessed=3_000_000, transcendentals=0)
VMEM = pl.BlockSpec(memory_space=pltpu.VMEM)
ANY = pl.BlockSpec(memory_space=pl.ANY)
SMEM = pl.BlockSpec(memory_space=pltpu.SMEM)


def row_table(rows, count):
    if count == rows:
        return [list(range(rows))]
    half = rows // 2
    middle = [0, half - 1, half, rows - 1]
    inner = [row for row in range(rows) if row not in middle]
    order = middle + inner
    return [order[c * count : (c + 1) * count] for c in range(rows // count)]


def pick(values, at):
    out = jnp.int32(values[0])
    for i, value in enumerate(values[1:], 1):
        out = jnp.where(at == i, jnp.int32(value), out)
    return out


def in_hbm(x):
    return pltpu.with_memory_space_constraint(x, pltpu.HBM)


def link_type(distance):
    return F32 if distance < 2 else BF16


def lateral(row):
    width = row.shape[1]
    lane = lax.broadcasted_iota(jnp.int32, row.shape, 1)
    left = jnp.where(lane == 0, 0.0, pltpu.roll(row, 1, 1))
    right = jnp.where(lane == width - 1, 0.0, pltpu.roll(row, width - 1, 1))
    return left + right


def dot(a, b):
    return jnp.dot(a, b, preferred_element_type=F32)


def halves(x):
    top = x.astype(BF16)
    return top, (x - top.astype(F32)).astype(BF16)


def by_row(x, rows, wanted, exact):
    levels = x.shape[0] // rows
    level = lax.broadcasted_iota(jnp.int32, (levels, x.shape[0]), 0)
    source = lax.broadcasted_iota(jnp.int32, (levels, x.shape[0]), 1)
    matrix = jnp.concatenate(
        [jnp.where(source == level * rows + row, 1.0, 0.0) for row in wanted], axis=0
    ).astype(BF16)
    if exact:
        out = dot(matrix, x)
    else:
        top, rest = halves(x)
        out = dot(matrix, top) + dot(matrix, rest)
    return {row: out[i * levels : (i + 1) * levels] for i, row in enumerate(wanted)}


def by_level(lines):
    rows, levels = len(lines), lines[0].shape[0]
    size = rows * levels
    target = lax.broadcasted_iota(jnp.int32, (size, levels), 0)
    level = lax.broadcasted_iota(jnp.int32, (size, levels), 1)
    matrix = jnp.concatenate(
        [jnp.where(target == level * rows + row, 1.0, 0.0) for row in range(rows)], axis=1
    ).astype(BF16)
    top, rest = halves(jnp.concatenate(lines, axis=0))
    return dot(jnp.concatenate([matrix, matrix], axis=1), jnp.concatenate([top, rest], axis=0))


def edge_rows_kernel(rows, state_ref, after_ref, first, last):
    lines = by_row(state_ref[...], rows, [0, rows - 1], True)
    first[...] = lines[0].astype(BF16)
    last[...] = lines[rows - 1].astype(BF16)


def edge_rows(state, after):
    fields, levels, rows, width = state.shape
    step = min(levels, 16)
    slab = pl.BlockSpec((None, step, width), lambda i, f: (f, i, 0))
    return pl.pallas_call(
        functools.partial(edge_rows_kernel, rows),
        out_shape=[jax.ShapeDtypeStruct((fields, levels, width), BF16)] * 2,
        grid=(levels // step, fields),
        in_specs=[pl.BlockSpec((None, step * rows, width), lambda i, f: (f, i, 0)), ANY],
        out_specs=[slab] * 2,
        compiler_params=PARAMS,
        cost_estimate=COST,
        name="edge_rows",
    )(in_hbm(state.reshape(fields, levels * rows, width)), after)


def split_kernel(table, count, rows, me_ref, cot_ref, *refs):
    outs, held = refs[: count - 1], refs[-1]
    me = me_ref[0]
    step = held.shape[1]
    here_at = pl.ds(pl.multiple_of(pl.program_id(0) * step, step), step)
    f = pl.program_id(1)
    lines = by_row(cot_ref[...], rows, list(range(rows)), True)
    for r in range(rows):
        held[r] = lines[r]
    for c, order in enumerate(table):
        for k in range(1, count):
            outs[k - 1][c, f, here_at, :] = held[pick(order, me ^ k)].astype(BF16)


def split_cot(me, cot, table, count):
    fields, levels, rows, width = cot.shape
    step = min(levels, 16)
    return pl.pallas_call(
        functools.partial(split_kernel, table, count, rows),
        out_shape=[pltpu.VMEM((len(table), fields, levels, width), BF16)] * (count - 1),
        grid=(levels // step, fields),
        in_specs=[SMEM, pl.BlockSpec((None, step * rows, width), lambda i, f: (f, i, 0))],
        out_specs=[VMEM] * (count - 1),
        scratch_shapes=[pltpu.VMEM((rows, step, width), F32)],
        compiler_params=PARAMS,
        cost_estimate=COST,
        name="split_cot",
    )(me, in_hbm(cot.reshape(fields, levels * rows, width)))


def transpose_kernel(v_ref, win_ref, wout_ref, after_ref, vt_ref, wint_ref, woutt_ref):
    for f in range(v_ref.shape[0]):
        vt_ref[f] = v_ref[f].T
    wint_ref[...] = win_ref[...].T
    woutt_ref[...] = wout_ref[...].T


def transposes(v, w_in, w_out, after):
    shapes = [(v.shape, F32), (w_in.shape[::-1], BF16), (w_out.shape[::-1], BF16)]
    return pl.pallas_call(
        transpose_kernel,
        out_shape=[pltpu.VMEM(dims, kind) for dims, kind in shapes],
        in_specs=[VMEM] * 3 + [ANY],
        out_specs=[VMEM] * 3,
        compiler_params=PARAMS,
        cost_estimate=COST,
        name="transposes",
    )(v, w_in, w_out, after)


def release_kernel(count, *refs):
    for source, target in zip(refs[:count], refs[-count:]):
        target[...] = source[...]


def release(pieces, after):
    return pl.pallas_call(
        functools.partial(release_kernel, len(pieces)),
        out_shape=[pltpu.VMEM(x.shape, x.dtype) for x in pieces],
        in_specs=[VMEM] * len(pieces) + [ANY] * len(after),
        out_specs=[VMEM] * len(pieces),
        compiler_params=PARAMS,
        cost_estimate=COST,
        name="release",
    )(*pieces, *after)


def forward_kernel(table, count, rows, me_ref, cot_ref, state_ref, diff_ref, low_ref, high_ref, *refs):
    own, diff_rows, *far, cot_rows, rows_held = refs[2:]
    me = me_ref[0]
    step = rows_held.shape[1]
    here_at = pl.ds(pl.multiple_of(pl.program_id(0) * step, step), step)
    f = pl.program_id(1)
    every = list(range(rows))
    lines = by_row(state_ref[...], rows, every, False)
    lines[-1] = low_ref[f, here_at, :].astype(F32)
    lines[rows] = high_ref[f, here_at, :].astype(F32)

    @pl.when(f == 0)
    def _():
        diff = by_row(diff_ref[...], rows, every, False)
        for r in every:
            diff_rows[r, here_at, :] = diff[r]

    cots = by_row(cot_ref[...], rows, every, True)
    for r in every:
        here = lines[r]
        total = lines[r - 1] + lines[r + 1] + lateral(here) - 4.0 * here
        rows_held[r] = here + diff_rows[r, here_at, :] * total
        cot_rows[r] = cots[r]
    for c, order in enumerate(table):
        for k in range(count):
            row = pick(order, me ^ k)
            if k == 0:
                own[c, 0, f, here_at, :] = cot_rows[row]
                own[c, 1, f, here_at, :] = rows_held[row]
            else:
                out = far[c * (count - 1) + k - 1]
                out[f, here_at, :] = rows_held[row].astype(out.dtype)


def forward(me, cot, state, diffusion, low, high, after, table, count):
    fields, levels, rows, width = state.shape
    step = min(levels, 16)
    chunks = len(table)
    shape = (fields, levels, width)
    outs = [(F32, (chunks, 2, *shape)), (F32, (rows, levels, width))]
    outs += [(link_type(k), shape) for _ in table for k in range(1, count)]
    tile = pl.BlockSpec((None, step * rows, width), lambda i, f: (f, i, 0))
    own, diff, *far = pl.pallas_call(
        functools.partial(forward_kernel, table, count, rows),
        out_shape=[pltpu.VMEM(dims, kind) for kind, dims in outs],
        grid=(levels // step, fields),
        in_specs=[SMEM, tile, tile]
        + [pl.BlockSpec((step * rows, width), lambda i, f: (i, 0))]
        + [VMEM] * 2
        + [ANY] * 2,
        out_specs=[VMEM] * len(outs),
        scratch_shapes=[pltpu.VMEM((rows, step, width), F32)] * 2,
        compiler_params=PARAMS,
        cost_estimate=COST,
        name="forward",
    )(
        me,
        in_hbm(cot.reshape(fields, levels * rows, width)),
        in_hbm(state.reshape(fields, levels * rows, width)),
        in_hbm(diffusion.reshape(levels * rows, width)),
        low,
        high,
        *after,
    )
    return own, diff, [far[c * (count - 1) : (c + 1) * (count - 1)] for c in range(chunks)]


def vertical(matrix, x):
    m_top, m_rest = halves(matrix)
    x_top, x_rest = halves(x)
    return dot(m_top, x_top) + (dot(m_rest, x_top) + dot(m_top, x_rest))


def column_kernel(count, at, tile, me_ref, own, *refs):
    far_cot, far = refs[: count - 1], refs[count - 1 : 2 * count - 2]
    v_ref, vt_ref, win_ref, wint_ref, woutt_ref = refs[2 * count - 2 : 2 * count + 3]
    outs, (cols, cot_cols, back) = refs[-count - 3 : -3], refs[-3:]
    fields, lev, _ = v_ref.shape
    me = me_ref[0]
    levels = lev // count
    lanes = pl.ds(pl.multiple_of(pl.program_id(0) * tile, tile), tile)
    for k in range(count):
        to = pl.ds(pl.multiple_of((me ^ k) * levels, levels), levels)
        for f in range(fields):
            if k == 0:
                cot, diffused = own[at, 0, f, :, lanes], own[at, 1, f, :, lanes]
            else:
                cot, diffused = far_cot[k - 1][at, f, :, lanes], far[k - 1][f, :, lanes]
            cot_cols[f, to, :] = cot.astype(F32)
            cols[f, to, :] = diffused.astype(F32)
    inputs = jnp.concatenate(
        [vertical(v_ref[f], cols[f]).astype(BF16) for f in range(fields)], axis=0
    )
    cot = jnp.concatenate([cot_cols[f] for f in range(fields)], axis=0)
    cot_half = cot.astype(BF16)
    hidden, block = win_ref.shape[0], 256
    grad = cot
    for h in range(0, hidden, block):
        preact = dot(win_ref[h : h + block, :], inputs)
        hidden_grad = dot(woutt_ref[h : h + block, :], cot_half)
        s = 0.5 + 0.5 * jnp.tanh(0.5 * preact)
        pre_grad = (hidden_grad * s * (1.0 + preact * (1.0 - s))).astype(BF16)
        grad = grad + dot(wint_ref[:, h : h + block], pre_grad)
    for f in range(fields):
        back[f] = vertical(vt_ref[f], grad[f * lev : (f + 1) * lev])
    for k in range(count):
        to = pl.ds(pl.multiple_of((me ^ k) * levels, levels), levels)
        for f in range(fields):
            outs[k][f, :, lanes] = back[f, to, :].astype(outs[k].dtype)


def columns(me, own, far_cot, far, at, v, vt, w_in, w_in_t, w_out_t, after, name):
    count = len(far) + 1
    *_, fields, levels, width = own.shape
    lev = v.shape[1]
    tile = min(width, 512)
    inputs = (own, *far_cot, *far, v, vt, w_in, w_in_t, w_out_t)
    return pl.pallas_call(
        functools.partial(column_kernel, count, at, tile),
        out_shape=[pltpu.VMEM((fields, levels, width), link_type(k)) for k in range(count)],
        grid=(width // tile,),
        in_specs=[SMEM] + [VMEM] * len(inputs) + [ANY] * len(after),
        out_specs=[VMEM] * count,
        scratch_shapes=[pltpu.VMEM((fields, lev, tile), F32)] * 3,
        compiler_params=PARAMS,
        cost_estimate=COST,
        name=name,
    )(me, *inputs, *after)


def edge_kernel(order, count, rows, me_ref, diff_ref, *refs):
    pieces, low, high = refs[:count], refs[count], refs[count + 1]
    me = me_ref[0]
    for k in range(count):
        row = pick(order, me ^ k)

        @pl.when(row == 0)
        def _():
            for f in range(low.shape[0]):
                low[f] = (diff_ref[0] * pieces[k][f].astype(F32)).astype(BF16)

        @pl.when(row == rows - 1)
        def _():
            for f in range(low.shape[0]):
                high[f] = (diff_ref[rows - 1] * pieces[k][f].astype(F32)).astype(BF16)


def edges(me, diff, pieces, order):
    rows, levels, width = diff.shape
    shape = pieces[0].shape
    return pl.pallas_call(
        functools.partial(edge_kernel, order, len(pieces), rows),
        out_shape=[pltpu.VMEM(shape, BF16)] * 2,
        in_specs=[SMEM] + [VMEM] * (1 + len(pieces)),
        out_specs=[VMEM] * 2,
        compiler_params=PARAMS,
        cost_estimate=COST,
        name="edges",
    )(me, diff, *pieces)


def final_kernel(table, count, rows, top, me_ref, diff_ref, low_ref, high_ref, pieces, out, held):
    me = me_ref[0]
    step, span, _ = out.shape
    start = top * span
    i, f = pl.program_id(0), pl.program_id(1)
    here_at = pl.ds(pl.multiple_of(i * step, step), step)
    for c, order in enumerate(table):
        for k in range(count):
            held[pick(order, me ^ k)] = pieces[c * count + k][f, here_at, :].astype(F32)

    def weighted(r):
        if r < 0:
            return low_ref[f, here_at, :].astype(F32)
        if r == rows:
            return high_ref[f, here_at, :].astype(F32)
        return held[r] * diff_ref[r, here_at, :]

    lines = []
    before, here = weighted(start - 1), weighted(start)
    for r in range(start, start + span):
        after = weighted(r + 1)
        lines.append(held[r] + before + after + lateral(here) - 4.0 * here)
        before, here = here, after
    out[...] = by_level(lines).reshape(out.shape)


def final(me, diff, low, high, pieces, table, top, base):
    count = len(pieces[0])
    fields, levels, width = low.shape
    rows = diff.shape[0]
    span = rows // 2
    step = min(levels, 16)
    needed = [piece for chunk in pieces for piece in chunk]
    aliased = [] if base is None else [base]

    def kernel(*refs):
        final_kernel(
            table[: len(pieces)], count, rows, top, *refs[:4], refs[4 : 4 + len(needed)], *refs[-2:]
        )

    return pl.pallas_call(
        kernel,
        out_shape=pltpu.HBM((fields, levels, rows, width), F32),
        grid=(levels // step, fields),
        in_specs=[SMEM] + [VMEM] * (3 + len(needed)) + [ANY] * len(aliased),
        out_specs=pl.BlockSpec((None, step, span, width), lambda i, f: (f, i, top, 0)),
        scratch_shapes=[pltpu.VMEM((rows, step, width), F32)],
        input_output_aliases={4 + len(needed): 0} if aliased else {},
        compiler_params=PARAMS,
        cost_estimate=COST,
        name=f"final_{top}",
    )(me, diff, low, high, *needed, *aliased)


def swap(x, distance, count):
    if distance == 0:
        return x
    return lax.ppermute(x, "lev", [(i, i ^ distance) for i in range(count)])


def halo(first, last):
    count = lax.axis_size("hor")
    forward = [(i, i + 1) for i in range(count - 1)]
    backward = [(target, source) for source, target in forward]
    return lax.ppermute(last, "hor", forward), lax.ppermute(first, "hor", backward)


def body(state, cotangent, diffusion, vertical_inverse, w_in, w_out):
    count = lax.axis_size("lev")
    rows = state.shape[2]
    table = row_table(rows, count)
    chunks = len(table)
    me = lax.axis_index("lev").astype(jnp.int32).reshape(1)
    split = split_cot(me, cotangent, table, count)
    far_cot = [swap(x, k, count) for k, x in enumerate(split, 1)]
    edge = edge_rows(state, split[0])
    low, high = halo(*edge)
    v_t, w_in_t, w_out_t = transposes(vertical_inverse, w_in, w_out, edge[0])
    weights = (vertical_inverse, v_t, w_in, w_in_t, w_out_t)
    after = [far_cot[0], w_in_t]
    own, diff, far = forward(me, cotangent, state, diffusion, low, high, after, table, count)
    returned, last = [], []

    def send(pieces):
        return [swap(x, k, count) for k, x in enumerate(pieces, 1)]

    moved = [send(pieces) for pieces in far[:2]]
    for c in range(chunks):
        if c + 2 < chunks:
            ready = release(far[c + 2], moved[c] + last)
            moved.append(send(ready))
            last = [ready[0]]
        out = columns(me, own, far_cot, moved[c], c, *weights, last, f"columns_{c}")
        last = [out[0]]
        returned.append([out[0]] + send(out[1:]))
    chunk_of = {row: c for c, order in enumerate(table) for row in order}
    edge = chunk_of[0]
    low, high = halo(*edges(me, diff, returned[edge], table[edge]))
    span = rows // 2
    needed = 1 + max(chunk_of[row] for row in range(span + 1))
    result = final(me, diff, low, high, returned[:needed], table, 0, None)
    return final(me, diff, low, high, returned, table, 1, result)


def solution(mesh):
    placed = (
        P(None, "lev", "hor", None),
        P(None, "lev", "hor", None),
        P("lev", "hor", None),
        P(),
        P(),
        P(),
    )
    return jax.shard_map(
        body, mesh=mesh, in_specs=placed, out_specs=P(None, "lev", "hor", None), check_vma=False
    )
```

```python
import functools

import jax
import jax.numpy as jnp
from jax import lax
from jax.experimental import pallas as pl
from jax.experimental.pallas import tpu as pltpu
from jax.sharding import PartitionSpec as P

F32, BF16 = jnp.float32, jnp.bfloat16
VMEM_MIB = 20
PARAMS = pltpu.CompilerParams(vmem_limit_bytes=VMEM_MIB * 1024 * 1024)
COST = pl.CostEstimate(flops=1, bytes_accessed=1, transcendentals=0)
COLUMN_COST = pl.CostEstimate(flops=6_000_000_000, bytes_accessed=1, transcendentals=0)
COLUMN_COST = pl.CostEstimate(flops=6_000_000_000, bytes_accessed=3_000_000, transcendentals=0)
VMEM = pl.BlockSpec(memory_space=pltpu.VMEM)
ANY = pl.BlockSpec(memory_space=pl.ANY)
SMEM = pl.BlockSpec(memory_space=pltpu.SMEM)


def row_table(rows, count):
    if count == rows:
        return [list(range(rows))]
    half = rows // 2
    middle = [0, half - 1, half, rows - 1]
    inner = [row for row in range(rows) if row not in middle]
    order = middle + inner
    return [order[c * count : (c + 1) * count] for c in range(rows // count)]


def pick(values, at):
    out = jnp.int32(values[0])
    for i, value in enumerate(values[1:], 1):
        out = jnp.where(at == i, jnp.int32(value), out)
    return out


def in_hbm(x):
    return pltpu.with_memory_space_constraint(x, pltpu.HBM)


def views(refs, pieces):
    return [ref if at is None else ref.at[at] for ref, (_, at) in zip(refs, pieces)]


def link_type(distance):
    return F32 if distance < 2 else BF16


def lateral(row):
    width = row.shape[1]
    lane = lax.broadcasted_iota(jnp.int32, row.shape, 1)
    left = jnp.where(lane == 0, 0.0, pltpu.roll(row, 1, 1))
    right = jnp.where(lane == width - 1, 0.0, pltpu.roll(row, width - 1, 1))
    return left + right


def dot(a, b):
    return jnp.dot(a, b, preferred_element_type=F32)


def halves(x):
    top = x.astype(BF16)
    return top, (x - top.astype(F32)).astype(BF16)


def by_row(x, rows, wanted, exact):
    levels = x.shape[0] // rows
    level = lax.broadcasted_iota(jnp.int32, (levels, x.shape[0]), 0)
    source = lax.broadcasted_iota(jnp.int32, (levels, x.shape[0]), 1)
    matrix = jnp.concatenate(
        [jnp.where(source == level * rows + row, 1.0, 0.0) for row in wanted], axis=0
    ).astype(BF16)
    if exact:
        out = dot(matrix, x)
    else:
        top, rest = halves(x)
        out = dot(matrix, top) + dot(matrix, rest)
    return {row: out[i * levels : (i + 1) * levels] for i, row in enumerate(wanted)}


def by_level(lines):
    rows, levels = len(lines), lines[0].shape[0]
    size = rows * levels
    target = lax.broadcasted_iota(jnp.int32, (size, levels), 0)
    level = lax.broadcasted_iota(jnp.int32, (size, levels), 1)
    matrix = jnp.concatenate(
        [jnp.where(target == level * rows + row, 1.0, 0.0) for row in range(rows)], axis=1
    ).astype(BF16)
    top, rest = halves(jnp.concatenate(lines, axis=0))
    return dot(jnp.concatenate([matrix, matrix], axis=1), jnp.concatenate([top, rest], axis=0))


def edge_rows_kernel(rows, state_ref, after_ref, first, last):
    lines = by_row(state_ref[...], rows, [0, rows - 1], True)
    first[...] = lines[0].astype(BF16)
    last[...] = lines[rows - 1].astype(BF16)


def edge_rows(state, after):
    fields, levels, rows, width = state.shape
    step = min(levels, 16)
    slab = pl.BlockSpec((None, step, width), lambda i, f: (f, i, 0))
    return pl.pallas_call(
        functools.partial(edge_rows_kernel, rows),
        out_shape=[jax.ShapeDtypeStruct((fields, levels, width), BF16)] * 2,
        grid=(levels // step, fields),
        in_specs=[pl.BlockSpec((None, step * rows, width), lambda i, f: (f, i, 0)), ANY],
        out_specs=[slab] * 2,
        compiler_params=PARAMS,
        cost_estimate=COST,
        name="edge_rows",
    )(in_hbm(state.reshape(fields, levels * rows, width)), after)


def split_kernel(table, count, rows, me_ref, cot_ref, *refs):
    outs, held = refs[: count - 1], refs[-1]
    me = me_ref[0]
    step = held.shape[1]
    here_at = pl.ds(pl.multiple_of(pl.program_id(0) * step, step), step)
    f = pl.program_id(1)
    lines = by_row(cot_ref[...], rows, list(range(rows)), True)
    for r in range(rows):
        held[r] = lines[r]
    for c, order in enumerate(table):
        for k in range(1, count):
            outs[k - 1][c, f, here_at, :] = held[pick(order, me ^ k)].astype(BF16)


def split_cot(me, cot, table, count):
    fields, levels, rows, width = cot.shape
    step = min(levels, 16)
    return pl.pallas_call(
        functools.partial(split_kernel, table, count, rows),
        out_shape=[pltpu.VMEM((len(table), fields, levels, width), BF16)] * (count - 1),
        grid=(levels // step, fields),
        in_specs=[SMEM, pl.BlockSpec((None, step * rows, width), lambda i, f: (f, i, 0))],
        out_specs=[VMEM] * (count - 1),
        scratch_shapes=[pltpu.VMEM((rows, step, width), F32)],
        compiler_params=PARAMS,
        cost_estimate=COST,
        name="split_cot",
    )(me, in_hbm(cot.reshape(fields, levels * rows, width)))


def transpose_kernel(v_ref, win_ref, wout_ref, after_ref, vt_ref, wint_ref, woutt_ref):
    for f in range(v_ref.shape[0]):
        vt_ref[f] = v_ref[f].T
    wint_ref[...] = win_ref[...].T
    woutt_ref[...] = wout_ref[...].T


def transposes(v, w_in, w_out, after):
    shapes = [(v.shape, F32), (w_in.shape[::-1], BF16), (w_out.shape[::-1], BF16)]
    return pl.pallas_call(
        transpose_kernel,
        out_shape=[pltpu.VMEM(dims, kind) for dims, kind in shapes],
        in_specs=[VMEM] * 3 + [ANY],
        out_specs=[VMEM] * 3,
        compiler_params=PARAMS,
        cost_estimate=COST,
        name="transposes",
    )(v, w_in, w_out, after)


def release_kernel(stacked, count, *refs):
    outs = refs[-count - bool(stacked) :]
    if stacked:
        outs = [outs[0].at[i] for i in range(stacked)] + list(outs[1:])
    for source, target in zip(refs, outs):
        target[...] = source[...]


def release(stack, pieces, after):
    shapes = [(x.shape, x.dtype) for x in pieces]
    if stack:
        shapes = [((len(stack), *stack[0].shape), stack[0].dtype)] + shapes
    return pl.pallas_call(
        functools.partial(release_kernel, len(stack), len(pieces)),
        out_shape=[pltpu.VMEM(*shape) for shape in shapes],
        in_specs=[VMEM] * (len(stack) + len(pieces)) + [ANY] * len(after),
        out_specs=[VMEM] * len(shapes),
        compiler_params=PARAMS,
        cost_estimate=COST,
        name="release",
    )(*stack, *pieces, *after)


def forward_kernel(table, count, rows, me_ref, cot_ref, state_ref, diff_ref, *refs):
    own_cot, diff_rows, edge, *out, cot_rows, rows_held = refs[1:]
    me = me_ref[0]
    step = rows_held.shape[1]
    here_at = pl.ds(pl.multiple_of(pl.program_id(0) * step, step), step)
    f = pl.program_id(1)
    every = list(range(rows))
    lines = by_row(state_ref[...], rows, every, False)
    lines[-1] = lines[rows] = jnp.zeros_like(lines[0])

    @pl.when(f == 0)
    def _():
        diff = by_row(diff_ref[...], rows, every, False)
        for r in every:
            diff_rows[r, here_at, :] = diff[r]

    cots = by_row(cot_ref[...], rows, every, True)
    for r in every:
        here = lines[r]
        total = lines[r - 1] + lines[r + 1] + lateral(here) - 4.0 * here
        rows_held[r] = here + diff_rows[r, here_at, :] * total
        cot_rows[r] = cots[r]
    for j, r in enumerate(table[0]):
        edge[j, f, here_at, :] = rows_held[r]
    for c, order in enumerate(table):
        own_cot[c, f, here_at, :] = cot_rows[pick(order, me)]
        for k in range(count if c else 0):
            to = out[(c - 1) * count + k]
            to[f, here_at, :] = rows_held[pick(order, me ^ k)].astype(to.dtype)


def forward(me, cot, state, diffusion, after, table, count):
    fields, levels, rows, width = state.shape
    step = min(levels, 16)
    chunks = len(table)
    shape = (fields, levels, width)
    outs = [(F32, (chunks, *shape)), (F32, (rows, levels, width)), (F32, (count, *shape))]
    outs += [(link_type(k), shape) for _ in table[1:] for k in range(count)]
    tile = pl.BlockSpec((None, step * rows, width), lambda i, f: (f, i, 0))
    own_cot, diff, edge, *out = pl.pallas_call(
        functools.partial(forward_kernel, table, count, rows),
        out_shape=[pltpu.VMEM(dims, kind) for kind, dims in outs],
        grid=(levels // step, fields),
        in_specs=[SMEM, tile, tile, pl.BlockSpec((step * rows, width), lambda i, f: (i, 0)), ANY],
        out_specs=[VMEM] * len(outs),
        scratch_shapes=[pltpu.VMEM((rows, step, width), F32)] * 2,
        compiler_params=PARAMS,
        cost_estimate=COST,
        name="forward",
    )(
        me,
        in_hbm(cot.reshape(fields, levels * rows, width)),
        in_hbm(state.reshape(fields, levels * rows, width)),
        in_hbm(diffusion.reshape(levels * rows, width)),
        after,
    )
    return own_cot, diff, edge, [out[c * count : (c + 1) * count] for c in range(chunks - 1)]


def halo_kernel(order, rows, others, me_ref, edge_ref, diff_ref, low_ref, high_ref, *refs):
    outs = list(refs[-len(order) :])
    me = me_ref[0]
    for k in range(1, len(order)):
        if others:
            outs[k][1] = refs[k - 1][...]
        outs[k] = outs[k].at[0]
    for f in range(low_ref.shape[0]):
        low = diff_ref[0] * low_ref[f].astype(F32)
        high = diff_ref[rows - 1] * high_ref[f].astype(F32)
        for k, out in enumerate(outs):
            row = pick(order, me ^ k)
            term = jnp.where(row == 0, low, jnp.where(row == rows - 1, high, 0.0))
            out[f] = (edge_ref[me ^ k, f] + term).astype(out.dtype)


def add_halo(me, edge, diff, low, high, others, after, order):
    shapes = [low.shape] + [(1 + bool(others), *low.shape)] * (len(order) - 1)
    return pl.pallas_call(
        functools.partial(halo_kernel, order, diff.shape[0], bool(others)),
        out_shape=[pltpu.VMEM(dims, link_type(k)) for k, dims in enumerate(shapes)],
        in_specs=[SMEM] + [VMEM] * (4 + len(others)) + [ANY] * len(after),
        out_specs=[VMEM] * len(order),
        compiler_params=PARAMS,
        cost_estimate=COST,
        name="add_halo",
    )(me, edge, diff, low, high, *others, *after)


def vertical(matrix, x):
    m_top, m_rest = halves(matrix)
    x_top, x_rest = halves(x)
    return dot(m_top, x_top) + (dot(m_rest, x_top) + dot(m_top, x_rest))


def column_kernel(count, at, tile, paired, places, me_ref, own_cot, *refs):
    far_cot, states = refs[: count - 1], views(refs[count - 1 : 2 * count - 1], places)
    v_ref, vt_ref, win_ref, wint_ref, woutt_ref = refs[2 * count - 1 : 2 * count + 4]
    outs, (cols, cot_cols, back) = refs[-count - 3 : -3], refs[-3:]
    fields, lev, _ = v_ref.shape
    me = me_ref[0]
    levels = lev // count
    lanes = pl.ds(pl.multiple_of(pl.program_id(0) * tile, tile), tile)
    for k in range(count):
        to = pl.ds(pl.multiple_of((me ^ k) * levels, levels), levels)
        for f in range(fields):
            cot = (far_cot[k - 1] if k else own_cot)[at, f, :, lanes]
            cot_cols[f, to, :] = cot.astype(F32)
            cols[f, to, :] = states[k][f, :, lanes].astype(F32)
    inputs = jnp.concatenate(
        [vertical(v_ref[f], cols[f]).astype(BF16) for f in range(fields)], axis=0
    )
    cot = jnp.concatenate([cot_cols[f] for f in range(fields)], axis=0)
    cot_half = cot.astype(BF16)
    hidden, block = win_ref.shape[0], 256
    grad = cot
    for h in range(0, hidden, block):
        preact = dot(win_ref[h : h + block, :], inputs)
        hidden_grad = dot(woutt_ref[h : h + block, :], cot_half)
        s = 0.5 + 0.5 * jnp.tanh(0.5 * preact)
        pre_grad = (hidden_grad * s * (1.0 + preact * (1.0 - s))).astype(BF16)
        grad = grad + dot(wint_ref[:, h : h + block], pre_grad)
    for f in range(fields):
        back[f] = vertical(vt_ref[f], grad[f * lev : (f + 1) * lev])
    for k in range(count):
        to = pl.ds(pl.multiple_of((me ^ k) * levels, levels), levels)
        for f in range(fields):
            value = back[f, to, :].astype(outs[k].dtype)
            if k == 1:
                outs[k][len(paired), f, :, lanes] = value
                for ref in paired:
                    outs[k][0, f, :, lanes] = refs[ref][0, f, :, lanes]
            else:
                outs[k][f, :, lanes] = value


def columns(me, own_cot, far_cot, states, at, v, vt, w_in, w_in_t, w_out_t, earlier, after, name):
    count = len(states)
    fields, levels, width = states[0][0].shape
    lev = v.shape[1]
    tile = min(width, 512)
    inputs = (own_cot, *far_cot, *[array for array, _ in states], v, vt, w_in, w_in_t, w_out_t, *earlier)
    shapes = [(fields, levels, width)] * count
    shapes[1] = (1 + len(earlier), *shapes[1])
    paired = [len(inputs) - 2] if earlier else []
    return pl.pallas_call(
        functools.partial(column_kernel, count, at, tile, paired, [(None, place) for _, place in states]),
        out_shape=[pltpu.VMEM(dims, link_type(k)) for k, dims in enumerate(shapes)],
        grid=(width // tile,),
        in_specs=[SMEM] + [VMEM] * len(inputs) + [ANY] * len(after),
        out_specs=[VMEM] * count,
        scratch_shapes=[pltpu.VMEM((fields, lev, tile), F32)] * 3,
        compiler_params=PARAMS,
        cost_estimate=COLUMN_COST,
        name=name,
    )(me, *inputs, *after)


def edge_kernel(order, rows, pieces, me_ref, diff_ref, *refs):
    count, (low, high) = len(order), refs[-2:]
    pieces = views(refs, pieces)
    me = me_ref[0]
    for k in range(count):
        row = pick(order, me ^ k)

        @pl.when(row == 0)
        def _():
            for f in range(low.shape[0]):
                low[f] = (diff_ref[0] * pieces[k][f].astype(F32)).astype(BF16)

        @pl.when(row == rows - 1)
        def _():
            for f in range(low.shape[0]):
                high[f] = (diff_ref[rows - 1] * pieces[k][f].astype(F32)).astype(BF16)


def edges(me, diff, pieces, order):
    rows = diff.shape[0]
    shape = pieces[0][0].shape
    return pl.pallas_call(
        functools.partial(edge_kernel, order, rows, [(None, at) for _, at in pieces]),
        out_shape=[pltpu.VMEM(shape, BF16)] * 2,
        in_specs=[SMEM] + [VMEM] * (1 + len(pieces)),
        out_specs=[VMEM] * 2,
        compiler_params=PARAMS,
        cost_estimate=COST,
        name="edges",
    )(me, diff, *[array for array, _ in pieces])


def final_kernel(table, count, rows, top, me_ref, diff_ref, low_ref, high_ref, pieces, out, held):
    me = me_ref[0]
    step, span, _ = out.shape
    start = top * span
    i, f = pl.program_id(0), pl.program_id(1)
    here_at = pl.ds(pl.multiple_of(i * step, step), step)
    for c, order in enumerate(table):
        for k in range(count):
            held[pick(order, me ^ k)] = pieces[c * count + k][f, here_at, :].astype(F32)

    def weighted(r):
        if r < 0:
            return low_ref[f, here_at, :].astype(F32)
        if r == rows:
            return high_ref[f, here_at, :].astype(F32)
        return held[r] * diff_ref[r, here_at, :]

    lines = []
    before, here = weighted(start - 1), weighted(start)
    for r in range(start, start + span):
        after = weighted(r + 1)
        lines.append(held[r] + before + after + lateral(here) - 4.0 * here)
        before, here = here, after
    out[...] = by_level(lines).reshape(out.shape)


def final(me, diff, low, high, pieces, table, top, base):
    count = len(pieces[0])
    fields, levels, width = low.shape
    rows = diff.shape[0]
    span = rows // 2
    step = min(levels, 16)
    needed = [piece for chunk in pieces for piece in chunk]
    aliased = [] if base is None else [base]

    def kernel(*refs):
        final_kernel(
            table[: len(pieces)], count, rows, top, *refs[:4], views(refs[4:], needed), *refs[-2:]
        )

    return pl.pallas_call(
        kernel,
        out_shape=pltpu.HBM((fields, levels, rows, width), F32),
        grid=(levels // step, fields),
        in_specs=[SMEM] + [VMEM] * (3 + len(needed)) + [ANY] * len(aliased),
        out_specs=pl.BlockSpec((None, step, span, width), lambda i, f: (f, i, top, 0)),
        scratch_shapes=[pltpu.VMEM((rows, step, width), F32)],
        input_output_aliases={4 + len(needed): 0} if aliased else {},
        compiler_params=PARAMS,
        cost_estimate=COST,
        name=f"final_{top}",
    )(me, diff, low, high, *[array for array, _ in needed], *aliased)


def swap(x, distance, count):
    if distance == 0:
        return x
    return lax.ppermute(x, "lev", [(i, i ^ distance) for i in range(count)])


def halo(first, last):
    count = lax.axis_size("hor")
    forward = [(i, i + 1) for i in range(count - 1)]
    backward = [(target, source) for source, target in forward]
    return lax.ppermute(last, "hor", forward), lax.ppermute(first, "hor", backward)


def body(state, cotangent, diffusion, vertical_inverse, w_in, w_out):
    count = lax.axis_size("lev")
    rows = state.shape[2]
    table = row_table(rows, count)
    chunks = len(table)
    me = lax.axis_index("lev").astype(jnp.int32).reshape(1)
    split = split_cot(me, cotangent, table, count)
    far_cot = [swap(x, k, count) for k, x in enumerate(split, 1)]
    sides = edge_rows(state, split[0])
    low, high = halo(*sides)
    v_t, w_in_t, w_out_t = transposes(vertical_inverse, w_in, w_out, sides[0])
    weights = (vertical_inverse, v_t, w_in, w_in_t, w_out_t)
    own_cot, diff, edge, diffused = forward(me, cotangent, state, diffusion, w_in_t, table, count)
    after = far_cot[:2]
    firsts = add_halo(me, edge, diff, low, high, sum((x[1:] for x in diffused[:1]), []), after, table[0])
    owns = [firsts[0]] + [x[0] for x in diffused]

    def send(pieces, first):
        return [swap(x, k, count) for k, x in enumerate(pieces, first)]

    firsts = send(firsts[1:], 1)
    arrived = [[(x, c) for x in firsts] for c in range(min(chunks, 2))]
    returned, last, near, pairs = [], [], [], []
    behind = [firsts[1], *far_cot[2:]]
    for c in range(chunks):
        if c + 2 < chunks:
            stack = [x[1] for x in diffused[c + 1 : c + 3]] if c % 2 == 0 else []
            ready = release(stack, diffused[c + 1][2:], behind + last)
            if stack:
                nears = swap(ready[0], 1, count)
            pieces = send(ready[bool(stack) :], 2)
            arrived.append([(nears, c % 2)] + [(x, None) for x in pieces])
            last = [ready[-1]]
            behind = [nears, pieces[0]]
        order = last
        if c == 2:
            pieces = returned[0][1:]
            order = last + pieces
        if c >= 3:
            if c == 3:
                pieces = [(x, None) for x in returned[0]]
                pieces.insert(1, pairs[0])
                low, high = halo(*edges(me, diff, pieces, table[0]))
            order = last + returned[c - 2][1:] + [low, high]
        out = columns(me, own_cot, far_cot, [(owns[c], None)] + arrived[c], c, *weights, near, order, f"columns_{c}")
        last = [out[0]]
        near = []
        if not near:
            moved_near = swap(out[1], 1, count)
            pairs += [(moved_near, i) for i in range(out[1].shape[0])]
        returned.append([out[0]] + send(out[2:], 2))
    for c, pieces in enumerate(returned):
        returned[c] = [(x, None) for x in pieces]
        returned[c].insert(1, pairs[c])
    chunk_of = {row: c for c, order in enumerate(table) for row in order}
    if chunks < 4:
        low, high = halo(*edges(me, diff, returned[0], table[0]))
    span = rows // 2
    needed = 1 + max(chunk_of[row] for row in range(span + 1))
    result = final(me, diff, low, high, returned[:needed], table, 0, None)
    return final(me, diff, low, high, returned, table, 1, result)


def solution(mesh):
    placed = (
        P(None, "lev", "hor", None),
        P(None, "lev", "hor", None),
        P("lev", "hor", None),
        P(),
        P(),
        P(),
    )
    return jax.shard_map(
        body, mesh=mesh, in_specs=placed, out_specs=P(None, "lev", "hor", None), check_vma=False
    )
```

```python
import functools

import jax
import jax.numpy as jnp
from jax import lax
from jax.experimental import pallas as pl
from jax.experimental.pallas import tpu as pltpu
from jax.sharding import PartitionSpec as P

F32, BF16 = jnp.float32, jnp.bfloat16
VMEM_MIB = 20
PARAMS = pltpu.CompilerParams(vmem_limit_bytes=VMEM_MIB * 1024 * 1024)
COST = pl.CostEstimate(flops=1, bytes_accessed=1, transcendentals=0)
COLUMN_COST = pl.CostEstimate(flops=4_000_000_000, bytes_accessed=1, transcendentals=0)
COLUMN_COST = pl.CostEstimate(flops=4_000_000_000, bytes_accessed=3_000_000, transcendentals=0)
VMEM = pl.BlockSpec(memory_space=pltpu.VMEM)
ANY = pl.BlockSpec(memory_space=pl.ANY)
SMEM = pl.BlockSpec(memory_space=pltpu.SMEM)


def row_table(rows, count):
    if count == rows:
        return [list(range(rows))]
    half = rows // 2
    middle = [0, half - 1, half, rows - 1]
    inner = [row for row in range(rows) if row not in middle]
    order = middle + inner
    return [order[c * count : (c + 1) * count] for c in range(rows // count)]


def pick(values, at):
    out = jnp.int32(values[0])
    for i, value in enumerate(values[1:], 1):
        out = jnp.where(at == i, jnp.int32(value), out)
    return out


def in_hbm(x):
    return pltpu.with_memory_space_constraint(x, pltpu.HBM)


def views(refs, pieces):
    return [ref if at is None else ref.at[at] for ref, (_, at) in zip(refs, pieces)]


def link_type(distance):
    return F32 if distance < 2 else BF16


def lateral(row):
    width = row.shape[1]
    lane = lax.broadcasted_iota(jnp.int32, row.shape, 1)
    left = jnp.where(lane == 0, 0.0, pltpu.roll(row, 1, 1))
    right = jnp.where(lane == width - 1, 0.0, pltpu.roll(row, width - 1, 1))
    return left + right


def dot(a, b):
    return jnp.dot(a, b, preferred_element_type=F32)


def halves(x):
    top = x.astype(BF16)
    return top, (x - top.astype(F32)).astype(BF16)


def by_row(x, rows, wanted, exact):
    levels = x.shape[0] // rows
    level = lax.broadcasted_iota(jnp.int32, (levels, x.shape[0]), 0)
    source = lax.broadcasted_iota(jnp.int32, (levels, x.shape[0]), 1)
    matrix = jnp.concatenate(
        [jnp.where(source == level * rows + row, 1.0, 0.0) for row in wanted], axis=0
    ).astype(BF16)
    if exact:
        out = dot(matrix, x)
    else:
        top, rest = halves(x)
        out = dot(matrix, top) + dot(matrix, rest)
    return {row: out[i * levels : (i + 1) * levels] for i, row in enumerate(wanted)}


def by_level(lines):
    rows, levels = len(lines), lines[0].shape[0]
    size = rows * levels
    target = lax.broadcasted_iota(jnp.int32, (size, levels), 0)
    level = lax.broadcasted_iota(jnp.int32, (size, levels), 1)
    matrix = jnp.concatenate(
        [jnp.where(target == level * rows + row, 1.0, 0.0) for row in range(rows)], axis=1
    ).astype(BF16)
    top, rest = halves(jnp.concatenate(lines, axis=0))
    return dot(jnp.concatenate([matrix, matrix], axis=1), jnp.concatenate([top, rest], axis=0))


def edge_rows_kernel(rows, state_ref, after_ref, first, last):
    lines = by_row(state_ref[...], rows, [0, rows - 1], True)
    first[...] = lines[0].astype(BF16)
    last[...] = lines[rows - 1].astype(BF16)


def edge_rows(state, after):
    fields, levels, rows, width = state.shape
    step = min(levels, 16)
    slab = pl.BlockSpec((None, step, width), lambda i, f: (f, i, 0))
    return pl.pallas_call(
        functools.partial(edge_rows_kernel, rows),
        out_shape=[jax.ShapeDtypeStruct((fields, levels, width), BF16)] * 2,
        grid=(levels // step, fields),
        in_specs=[pl.BlockSpec((None, step * rows, width), lambda i, f: (f, i, 0)), ANY],
        out_specs=[slab] * 2,
        compiler_params=PARAMS,
        cost_estimate=COST,
        name="edge_rows",
    )(in_hbm(state.reshape(fields, levels * rows, width)), after)


def split_kernel(table, count, rows, me_ref, cot_ref, *refs):
    outs, held = refs[: count - 1], refs[-1]
    me = me_ref[0]
    step = held.shape[1]
    here_at = pl.ds(pl.multiple_of(pl.program_id(0) * step, step), step)
    f = pl.program_id(1)
    lines = by_row(cot_ref[...], rows, list(range(rows)), True)
    for r in range(rows):
        held[r] = lines[r]
    for c, order in enumerate(table):
        for k in range(1, count):
            outs[k - 1][c, f, here_at, :] = held[pick(order, me ^ k)].astype(BF16)


def split_cot(me, cot, table, count):
    fields, levels, rows, width = cot.shape
    step = min(levels, 16)
    return pl.pallas_call(
        functools.partial(split_kernel, table, count, rows),
        out_shape=[pltpu.VMEM((len(table), fields, levels, width), BF16)] * (count - 1),
        grid=(levels // step, fields),
        in_specs=[SMEM, pl.BlockSpec((None, step * rows, width), lambda i, f: (f, i, 0))],
        out_specs=[VMEM] * (count - 1),
        scratch_shapes=[pltpu.VMEM((rows, step, width), F32)],
        compiler_params=PARAMS,
        cost_estimate=COST,
        name="split_cot",
    )(me, in_hbm(cot.reshape(fields, levels * rows, width)))


def transpose_kernel(v_ref, win_ref, wout_ref, after_ref, vt_ref, wint_ref, woutt_ref):
    for f in range(v_ref.shape[0]):
        vt_ref[f] = v_ref[f].T
    wint_ref[...] = win_ref[...].T
    woutt_ref[...] = wout_ref[...].T


def transposes(v, w_in, w_out, after):
    shapes = [(v.shape, F32), (w_in.shape[::-1], BF16), (w_out.shape[::-1], BF16)]
    return pl.pallas_call(
        transpose_kernel,
        out_shape=[pltpu.VMEM(dims, kind) for dims, kind in shapes],
        in_specs=[VMEM] * 3 + [ANY],
        out_specs=[VMEM] * 3,
        compiler_params=PARAMS,
        cost_estimate=COST,
        name="transposes",
    )(v, w_in, w_out, after)


def release_kernel(stacked, count, *refs):
    outs = refs[-count - bool(stacked) :]
    if stacked:
        outs = [outs[0].at[i] for i in range(stacked)] + list(outs[1:])
    for source, target in zip(refs, outs):
        target[...] = source[...]


def release(stack, pieces, after):
    shapes = [(x.shape, x.dtype) for x in pieces]
    if stack:
        shapes = [((len(stack), *stack[0].shape), stack[0].dtype)] + shapes
    return pl.pallas_call(
        functools.partial(release_kernel, len(stack), len(pieces)),
        out_shape=[pltpu.VMEM(*shape) for shape in shapes],
        in_specs=[VMEM] * (len(stack) + len(pieces)) + [ANY] * len(after),
        out_specs=[VMEM] * len(shapes),
        compiler_params=PARAMS,
        cost_estimate=COST,
        name="release",
    )(*stack, *pieces, *after)


def forward_kernel(table, count, rows, me_ref, cot_ref, state_ref, diff_ref, *refs):
    own_cot, diff_rows, edge, *out, cot_rows, rows_held = refs[1:]
    me = me_ref[0]
    step = rows_held.shape[1]
    here_at = pl.ds(pl.multiple_of(pl.program_id(0) * step, step), step)
    f = pl.program_id(1)
    every = list(range(rows))
    lines = by_row(state_ref[...], rows, every, False)
    lines[-1] = lines[rows] = jnp.zeros_like(lines[0])

    @pl.when(f == 0)
    def _():
        diff = by_row(diff_ref[...], rows, every, False)
        for r in every:
            diff_rows[r, here_at, :] = diff[r]

    cots = by_row(cot_ref[...], rows, every, True)
    for r in every:
        here = lines[r]
        total = lines[r - 1] + lines[r + 1] + lateral(here) - 4.0 * here
        rows_held[r] = here + diff_rows[r, here_at, :] * total
        cot_rows[r] = cots[r]
    for j, r in enumerate(table[0]):
        edge[j, f, here_at, :] = rows_held[r]
    for c, order in enumerate(table):
        own_cot[c, f, here_at, :] = cot_rows[pick(order, me)]
        for k in range(count if c else 0):
            to = out[(c - 1) * count + k]
            to[f, here_at, :] = rows_held[pick(order, me ^ k)].astype(to.dtype)


def forward(me, cot, state, diffusion, after, table, count):
    fields, levels, rows, width = state.shape
    step = min(levels, 16)
    chunks = len(table)
    shape = (fields, levels, width)
    outs = [(F32, (chunks, *shape)), (F32, (rows, levels, width)), (F32, (count, *shape))]
    outs += [(link_type(k), shape) for _ in table[1:] for k in range(count)]
    tile = pl.BlockSpec((None, step * rows, width), lambda i, f: (f, i, 0))
    own_cot, diff, edge, *out = pl.pallas_call(
        functools.partial(forward_kernel, table, count, rows),
        out_shape=[pltpu.VMEM(dims, kind) for kind, dims in outs],
        grid=(levels // step, fields),
        in_specs=[SMEM, tile, tile, pl.BlockSpec((step * rows, width), lambda i, f: (i, 0)), ANY],
        out_specs=[VMEM] * len(outs),
        scratch_shapes=[pltpu.VMEM((rows, step, width), F32)] * 2,
        compiler_params=PARAMS,
        cost_estimate=COST,
        name="forward",
    )(
        me,
        in_hbm(cot.reshape(fields, levels * rows, width)),
        in_hbm(state.reshape(fields, levels * rows, width)),
        in_hbm(diffusion.reshape(levels * rows, width)),
        after,
    )
    return own_cot, diff, edge, [out[c * count : (c + 1) * count] for c in range(chunks - 1)]


def halo_kernel(order, rows, others, me_ref, edge_ref, diff_ref, low_ref, high_ref, *refs):
    outs = list(refs[-len(order) :])
    me = me_ref[0]
    for k in range(1, len(order)):
        if others:
            outs[k][1] = refs[k - 1][...]
        outs[k] = outs[k].at[0]
    for f in range(low_ref.shape[0]):
        low = diff_ref[0] * low_ref[f].astype(F32)
        high = diff_ref[rows - 1] * high_ref[f].astype(F32)
        for k, out in enumerate(outs):
            row = pick(order, me ^ k)
            term = jnp.where(row == 0, low, jnp.where(row == rows - 1, high, 0.0))
            out[f] = (edge_ref[me ^ k, f] + term).astype(out.dtype)


def add_halo(me, edge, diff, low, high, others, after, order):
    shapes = [low.shape] + [(1 + bool(others), *low.shape)] * (len(order) - 1)
    return pl.pallas_call(
        functools.partial(halo_kernel, order, diff.shape[0], bool(others)),
        out_shape=[pltpu.VMEM(dims, link_type(k)) for k, dims in enumerate(shapes)],
        in_specs=[SMEM] + [VMEM] * (4 + len(others)) + [ANY] * len(after),
        out_specs=[VMEM] * len(order),
        compiler_params=PARAMS,
        cost_estimate=COST,
        name="add_halo",
    )(me, edge, diff, low, high, *others, *after)


def vertical(matrix, x):
    m_top, m_rest = halves(matrix)
    x_top, x_rest = halves(x)
    return dot(m_top, x_top) + (dot(m_rest, x_top) + dot(m_top, x_rest))


def column_kernel(count, at, tile, places, me_ref, own_cot, *refs):
    far_cot, states = refs[: count - 1], views(refs[count - 1 : 2 * count - 1], places)
    v_ref, vt_ref, win_ref, wint_ref, woutt_ref = refs[2 * count - 1 : 2 * count + 4]
    outs, (cols, cot_cols, back) = refs[-count - 3 : -3], refs[-3:]
    fields, lev, _ = v_ref.shape
    me = me_ref[0]
    levels = lev // count
    lanes = pl.ds(pl.multiple_of(pl.program_id(0) * tile, tile), tile)
    for k in range(count):
        to = pl.ds(pl.multiple_of((me ^ k) * levels, levels), levels)
        for f in range(fields):
            cot = (far_cot[k - 1] if k else own_cot)[at, f, :, lanes]
            cot_cols[f, to, :] = cot.astype(F32)
            cols[f, to, :] = states[k][f, :, lanes].astype(F32)
    inputs = jnp.concatenate(
        [vertical(v_ref[f], cols[f]).astype(BF16) for f in range(fields)], axis=0
    )
    cot = jnp.concatenate([cot_cols[f] for f in range(fields)], axis=0)
    cot_half = cot.astype(BF16)
    hidden, block = win_ref.shape[0], 512
    grad = cot
    for h in range(0, hidden, block):
        preact = dot(win_ref[h : h + block, :], inputs)
        hidden_grad = dot(woutt_ref[h : h + block, :], cot_half)
        s = 0.5 + 0.5 * jnp.tanh(0.5 * preact)
        pre_grad = (hidden_grad * s * (1.0 + preact * (1.0 - s))).astype(BF16)
        grad = grad + dot(wint_ref[:, h : h + block], pre_grad)
    for f in range(fields):
        back[f] = vertical(vt_ref[f], grad[f * lev : (f + 1) * lev])
    for k in range(count):
        to = pl.ds(pl.multiple_of((me ^ k) * levels, levels), levels)
        for f in range(fields):
            outs[k][f, :, lanes] = back[f, to, :].astype(outs[k].dtype)


def columns(me, own_cot, far_cot, states, at, v, vt, w_in, w_in_t, w_out_t, after, name):
    count = len(states)
    fields, levels, width = states[0][0].shape
    lev = v.shape[1]
    tile = min(width, 1024)
    inputs = (own_cot, *far_cot, *[array for array, _ in states], v, vt, w_in, w_in_t, w_out_t)
    return pl.pallas_call(
        functools.partial(column_kernel, count, at, tile, [(None, place) for _, place in states]),
        out_shape=[pltpu.VMEM((fields, levels, width), link_type(k)) for k in range(count)],
        grid=(width // tile,),
        in_specs=[SMEM] + [VMEM] * len(inputs) + [ANY] * len(after),
        out_specs=[VMEM] * count,
        scratch_shapes=[pltpu.VMEM((fields, lev, tile), F32)] * 3,
        compiler_params=PARAMS,
        cost_estimate=COLUMN_COST,
        name=name,
    )(me, *inputs, *after)


def edge_kernel(order, rows, me_ref, diff_ref, *refs):
    count, (low, high) = len(order), refs[-2:]
    pieces = refs[:count]
    me = me_ref[0]
    for k in range(count):
        row = pick(order, me ^ k)

        @pl.when(row == 0)
        def _():
            for f in range(low.shape[0]):
                low[f] = (diff_ref[0] * pieces[k][f].astype(F32)).astype(BF16)

        @pl.when(row == rows - 1)
        def _():
            for f in range(low.shape[0]):
                high[f] = (diff_ref[rows - 1] * pieces[k][f].astype(F32)).astype(BF16)


def edges(me, diff, pieces, order):
    rows = diff.shape[0]
    shape = pieces[0].shape
    return pl.pallas_call(
        functools.partial(edge_kernel, order, rows),
        out_shape=[pltpu.VMEM(shape, BF16)] * 2,
        in_specs=[SMEM] + [VMEM] * (1 + len(pieces)),
        out_specs=[VMEM] * 2,
        compiler_params=PARAMS,
        cost_estimate=COST,
        name="edges",
    )(me, diff, *pieces)


def final_kernel(table, count, rows, top, me_ref, diff_ref, low_ref, high_ref, pieces, out, held):
    me = me_ref[0]
    step, span, _ = out.shape
    start = top * span
    i, f = pl.program_id(0), pl.program_id(1)
    here_at = pl.ds(pl.multiple_of(i * step, step), step)
    for c, order in enumerate(table):
        for k in range(count):
            held[pick(order, me ^ k)] = pieces[c * count + k][f, here_at, :].astype(F32)

    def weighted(r):
        if r < 0:
            return low_ref[f, here_at, :].astype(F32)
        if r == rows:
            return high_ref[f, here_at, :].astype(F32)
        return held[r] * diff_ref[r, here_at, :]

    lines = []
    before, here = weighted(start - 1), weighted(start)
    for r in range(start, start + span):
        after = weighted(r + 1)
        lines.append(held[r] + before + after + lateral(here) - 4.0 * here)
        before, here = here, after
    out[...] = by_level(lines).reshape(out.shape)


def final(me, diff, low, high, pieces, table, top, base):
    count = len(pieces[0])
    fields, levels, width = low.shape
    rows = diff.shape[0]
    span = rows // 2
    step = min(levels, 16)
    needed = [piece for chunk in pieces for piece in chunk]
    aliased = [] if base is None else [base]

    def kernel(*refs):
        final_kernel(
            table[: len(pieces)], count, rows, top, *refs[:4], refs[4 : 4 + len(needed)], *refs[-2:]
        )

    return pl.pallas_call(
        kernel,
        out_shape=pltpu.HBM((fields, levels, rows, width), F32),
        grid=(levels // step, fields),
        in_specs=[SMEM] + [VMEM] * (3 + len(needed)) + [ANY] * len(aliased),
        out_specs=pl.BlockSpec((None, step, span, width), lambda i, f: (f, i, top, 0)),
        scratch_shapes=[pltpu.VMEM((rows, step, width), F32)],
        input_output_aliases={4 + len(needed): 0} if aliased else {},
        compiler_params=PARAMS,
        cost_estimate=COST,
        name=f"final_{top}",
    )(me, diff, low, high, *needed, *aliased)


def swap(x, distance, count):
    if distance == 0:
        return x
    return lax.ppermute(x, "lev", [(i, i ^ distance) for i in range(count)])


def halo(first, last):
    count = lax.axis_size("hor")
    forward = [(i, i + 1) for i in range(count - 1)]
    backward = [(target, source) for source, target in forward]
    return lax.ppermute(last, "hor", forward), lax.ppermute(first, "hor", backward)


def body(state, cotangent, diffusion, vertical_inverse, w_in, w_out):
    count = lax.axis_size("lev")
    rows = state.shape[2]
    table = row_table(rows, count)
    chunks = len(table)
    me = lax.axis_index("lev").astype(jnp.int32).reshape(1)
    split = split_cot(me, cotangent, table, count)
    far_cot = [swap(x, k, count) for k, x in enumerate(split, 1)]
    sides = edge_rows(state, split[0])
    low, high = halo(*sides)
    v_t, w_in_t, w_out_t = transposes(vertical_inverse, w_in, w_out, sides[0])
    weights = (vertical_inverse, v_t, w_in, w_in_t, w_out_t)
    own_cot, diff, edge, diffused = forward(me, cotangent, state, diffusion, w_in_t, table, count)
    after = far_cot[:2]
    firsts = add_halo(me, edge, diff, low, high, sum((x[1:] for x in diffused[:1]), []), after, table[0])
    owns = [firsts[0]] + [x[0] for x in diffused]

    def send(pieces, first):
        return [swap(x, k, count) for k, x in enumerate(pieces, first)]

    firsts = send(firsts[1:], 1)
    arrived = [[(x, c) for x in firsts] for c in range(min(chunks, 2))]
    returned, last = [], []
    behind = [firsts[1], *far_cot[2:]]
    for c in range(chunks):
        if c + 2 < chunks:
            stack = [x[1] for x in diffused[c + 1 : c + 3]] if c % 2 == 0 else []
            ready = release(stack, diffused[c + 1][2:], behind + last)
            if stack:
                nears = swap(ready[0], 1, count)
            pieces = send(ready[bool(stack) :], 2)
            arrived.append([(nears, c % 2)] + [(x, None) for x in pieces])
            last = [ready[-1]]
            behind = [nears, pieces[0]]
        order = last
        if c == 2:
            order = last + returned[0][2:]
        if c >= 3:
            if c == 3:
                low, high = halo(*edges(me, diff, returned[0], table[0]))
            order = last + returned[c - 2][2:] + [low, high]
        states = [(owns[c], None)] + arrived[c]
        out = columns(me, own_cot, far_cot, states, c, *weights, order, f"columns_{c}")
        last = [out[0]]
        returned.append([out[0]] + send(out[1:], 1))
    chunk_of = {row: c for c, order in enumerate(table) for row in order}
    if chunks < 4:
        low, high = halo(*edges(me, diff, returned[0], table[0]))
    span = rows // 2
    needed = 1 + max(chunk_of[row] for row in range(span + 1))
    result = final(me, diff, low, high, returned[:needed], table, 0, None)
    return final(me, diff, low, high, returned, table, 1, result)


def solution(mesh):
    placed = (
        P(None, "lev", "hor", None),
        P(None, "lev", "hor", None),
        P("lev", "hor", None),
        P(),
        P(),
        P(),
    )
    return jax.shard_map(
        body, mesh=mesh, in_specs=placed, out_specs=P(None, "lev", "hor", None), check_vma=False
    )
```
